256 devices in a mesh: tm: 16 (over y_lo, x, core), space: 16 (over z, y_hi).
Axes of the slice: x: 4, y: 4 (y_hi: 2, y_lo: 2; y = y_hi * 2 + y_lo), z: 8, core: 2. Of those that a mesh axis runs over, the one named last changes fastest.
Arguments:
- sources: float32 [192, 64, 32, 128], P('tm', None, 'space'), may hold values from -6 to 6
- fine_volume: float32 [64, 64], replicated
- fine_faces: float32 [6, 2, 64, 64], replicated
- coarse_volume: float32 [64, 64], replicated
- coarse_faces: float32 [6, 2, 64, 64], replicated
- flow_kinds: int32 [6, 32, 128], P(None, 'space'), may hold values from 0 to 1
- neighbours: int32 [4, 128], replicated, may hold values from 0 to 127, as said below
Outputs:
- iterate: float32 [192, 64, 32, 128], P('tm', None, 'space')
The draws below stay inside these ranges and needn't reach their ends.
Inputs may be any that keep to these rules, and one draw needn't show every extreme that they name: `neighbours`: row f lists, for each element, the element beside it across side face f of a periodic 8 x 16 grid of elements whose labels are shuffled; rows 0 and 1 are opposite faces, as are rows 2 and 3, and each row names every element once.
All inputs are finite; a program needn't handle non-finite values.
Results may differ from the reference program's by a relative error of at most 0.0001.
Values sent between devices are 32-bit elements; how exact they have to be, the bound alone decides.
A program may use at most 64 MiB of HBM per device.

```python
import jax
import jax.numpy as jnp
from jax import lax

NODES = 64
CF = 4
PLANE_X = 8
PLANE_Y = 16
PLANE = 128
LAYERS = 32
NT = 192


def block_from(diag_key, noise, lower, upper, power):
    spread = jax.random.uniform(diag_key, (NODES,), jnp.float32, 0.0, 1.0)
    diagonal = lower + (upper - lower) * spread ** power
    return jnp.diag(diagonal) + noise


def faces_from(plane, noise, below_key, above_key, below_lo, below_hi, power):
    below_spread = jax.random.uniform(below_key, (2, NODES), jnp.float32, 0.0, 1.0)
    above_spread = jax.random.uniform(above_key, (2, NODES), jnp.float32, 0.0, 1.0)
    below_diag = below_lo + (below_hi - below_lo) * below_spread ** power
    above_diag = 0.005 + 0.01 * above_spread ** power
    identity = jnp.eye(NODES, dtype=jnp.float32)
    below_block = below_diag[:, :, None] * identity[None] + noise[0]
    above_block = above_diag[:, :, None] * identity[None] + 0.35 * noise[1]
    vertical = jnp.stack([below_block, above_block], 0)
    return jnp.concatenate([plane, vertical], 0)


def draw_fine_volume(key, part):
    key = jax.random.fold_in(key, 1)
    diag_key, noise_key = jax.random.split(key)
    noise = 0.0025 * jax.random.normal(noise_key, (NODES, NODES), jnp.float32)
    return block_from(diag_key, noise, 0.8, 0.85, 1.0)


def draw_coarse_volume(key, part):
    key = jax.random.fold_in(key, 2)
    diag_key, noise_key = jax.random.split(key)
    noise = 0.002 * jax.random.normal(noise_key, (NODES, NODES), jnp.float32)
    return block_from(diag_key, noise, 0.74, 0.82, 1.0)


def draw_fine_faces(key, part):
    key = jax.random.fold_in(key, 3)
    plane_key, below_key, above_key, noise_key = jax.random.split(key, 4)
    plane = 0.0007 * jax.random.normal(plane_key, (4, 2, NODES, NODES), jnp.float32)
    noise = 0.002 * jax.random.normal(noise_key, (2, 2, NODES, NODES), jnp.float32)
    return faces_from(plane, noise, below_key, above_key, 0.05, 0.08, 1.0)


def draw_coarse_faces(key, part):
    key = jax.random.fold_in(key, 4)
    plane_key, below_key, above_key, noise_key = jax.random.split(key, 4)
    plane = 0.0007 * jax.random.normal(plane_key, (4, 2, NODES, NODES), jnp.float32)
    noise = 0.002 * jax.random.normal(noise_key, (2, 2, NODES, NODES), jnp.float32)
    return faces_from(plane, noise, below_key, above_key, 0.06, 0.1, 1.0)


def draw_neighbours(key, part):
    key = jax.random.fold_in(key, 5)
    count = PLANE_X * PLANE_Y
    labels = jax.random.permutation(key, count).astype(jnp.int32)
    places = jnp.argsort(labels).astype(jnp.int32)
    row_pos = places // PLANE_Y
    col_pos = places % PLANE_Y
    targets = [(row_pos + 1) % PLANE_X * PLANE_Y + col_pos, (row_pos + PLANE_X - 1) % PLANE_X * PLANE_Y + col_pos, row_pos * PLANE_Y + (col_pos + 1) % PLANE_Y, row_pos * PLANE_Y + (col_pos + PLANE_Y - 1) % PLANE_Y]
    return jnp.stack([labels[target] for target in targets], 0).astype(jnp.int32)


def with_ends(drawn, stream_key, least, largest):
    spot = [jax.random.randint(jax.random.fold_in(stream_key, axis), (), 0, length) for axis, length in enumerate(drawn.shape)]
    widest = drawn.shape.index(max(drawn.shape))
    neighbour = spot[:widest] + [(spot[widest] + 1) % drawn.shape[widest]] + spot[widest + 1:]
    return drawn.at[tuple(spot)].set(least).at[tuple(neighbour)].set(largest)


def block_levels(key, dims, shards, least, largest):
    def one(axis_at, shards_of):
        draws = jax.random.uniform(jax.random.fold_in(jax.random.fold_in(key, 6), axis_at), (shards_of,), jnp.float32, least / len(shards), largest / len(shards))
        return jnp.repeat(jnp.exp(draws), dims[axis_at] // shards_of).reshape((-1,) + (1,) * (len(dims) - axis_at - 1))

    level = one(*shards[0])
    for cut in shards[1:]:
        level = level * one(*cut)
    return level


def gaussian(stream_key, shape, scale, reach, cuts=(), kind=jnp.bfloat16):
    array = scale * jax.random.normal(stream_key, shape, jnp.float32)
    if cuts:
        array = array * block_levels(stream_key, shape, cuts, -0.22, 0.18)
    return jnp.clip(array, -reach, reach).astype(kind)


def setup_inputs(seed: int = 0) -> dict:
    keys = jax.random.split(jax.random.key(seed), 8)
    sources = gaussian(keys[0], (NT, NODES, LAYERS, PLANE), 1.0, 6.0, ((0, 16), (2, 16)), jnp.float32)
    fine_volume = draw_fine_volume(jax.random.fold_in(keys[7], 71), 0)
    fine_faces = draw_fine_faces(jax.random.fold_in(keys[7], 71), 0)
    coarse_volume = draw_coarse_volume(jax.random.fold_in(keys[7], 71), 0)
    coarse_faces = draw_coarse_faces(jax.random.fold_in(keys[7], 71), 0)
    flow_kinds = with_ends(jax.random.randint(keys[5], (6, LAYERS, PLANE), 0, 2), jax.random.fold_in(keys[5], 1), 0, 1).astype(jnp.int32)
    neighbours = draw_neighbours(jax.random.fold_in(keys[7], 71), 0)
    return {"sources": sources, "fine_volume": fine_volume, "fine_faces": fine_faces, "coarse_volume": coarse_volume, "coarse_faces": coarse_faces, "flow_kinds": flow_kinds, "neighbours": neighbours}


highest = lax.Precision.HIGHEST


def advance(field, volume, faces_op, flow_kinds, neighbours):
    result = jnp.einsum('ab,jbzp->jazp', volume, field, precision=highest)
    for face_id in range(4):
        pair_prod = jnp.einsum('kab,jbzp->kjazp', faces_op[face_id], field, precision=highest)
        shifted = jnp.take(pair_prod, neighbours[face_id], axis=4)
        result = result + jnp.where(flow_kinds[face_id] == 1, shifted[1], shifted[0])
    padded = jnp.pad(field, ((0, 0), (0, 0), (1, 1), (0, 0)))
    layer_count = field.shape[2]
    for face_id, offset in ((4, 0), (5, 2)):
        pair_prod = jnp.einsum('kab,jbzp->kjazp', faces_op[face_id], padded[:, :, offset:offset + layer_count], precision=highest)
        result = result + jnp.where(flow_kinds[face_id] == 1, pair_prod[1], pair_prod[0])
    return result


def reference(sources, fine_volume, fine_faces, coarse_volume, coarse_faces, flow_kinds, neighbours):
    tail = sources.shape[1:]
    intervals = sources.shape[0] // CF
    forcing = sources.reshape((intervals, CF) + tail)

    def fine_step(field):
        return advance(field, fine_volume, fine_faces, flow_kinds, neighbours)

    def relax(c_states):
        current = c_states
        states = [current]
        for inner in range(1, CF):
            current = fine_step(current) + forcing[:, inner]
            states.append(current)
        return jnp.stack(states, 1)

    def earlier(fine_all):
        lasts = fine_all[:, CF - 1]
        return jnp.concatenate([jnp.zeros((1,) + tail, jnp.float32), lasts[:-1]], 0)

    c_states = jnp.zeros((intervals,) + tail, jnp.float32)
    fine_all = relax(c_states)
    c_states = fine_step(earlier(fine_all)) + forcing[:, 0]
    fine_all = relax(c_states)
    residue = fine_step(earlier(fine_all)) + forcing[:, 0] - c_states

    def chain_step(current, term):
        following = advance(current[None], coarse_volume, coarse_faces, flow_kinds, neighbours)[0] + term
        return following, following

    final_state, correction = lax.scan(chain_step, jnp.zeros(tail, jnp.float32), residue)
    fine_all = relax(c_states + correction)
    return fine_all.reshape(sources.shape)
```

```python
import jax
import jax.numpy as jnp
from jax import lax
from jax.experimental import pallas as pl
from jax.experimental.pallas import tpu as pltpu
from jax.sharding import PartitionSpec as P

CF = 4
NODES = 64
PLANE = 128
OWN = 2
KH = 4
MESH = pl.DeviceIdType.MESH
f32, bf16 = jnp.float32, jnp.bfloat16


def dot(a, b):
    return jnp.dot(a, b, preferred_element_type=f32)


def split(value):
    high = value.astype(bf16)
    low = (value - high.astype(f32)).astype(bf16)
    return high, low


def span(halo, d):
    low = halo - OWN * d
    first, last = max(low, 0), min(low + OWN, OWN + 2 * halo)
    return first, last - first, first - low


def kernel(sections, positions, layers, intervals,
           x_ref, fv_ref, ff_ref, cv_ref, cf_ref, kinds_ref, nb_ref, out_ref,
           fine_op, coarse_op, kwin, idx, w0, w1, w2, w3, aout, ain, ww, rw0, rw1, r2, lout, ein, eout,
           send_sem, recv_sem):
    tm, sp = lax.axis_index("tm"), lax.axis_index("space")

    def at(d, ahead):
        return (lax.rem(tm + ahead + sections, sections), lax.rem(sp + d + positions, positions))

    partners = [at(d, 0) for d in (-3, -2, -1, 1, 2, 3)]
    partners += [at(d, a) for a in (-1, 1) for d in range(-3, 4)]
    barrier = pltpu.get_barrier_semaphore()
    for device in partners:
        pl.semaphore_signal(barrier, inc=1, device_id=device, device_id_type=MESH)

    def source(t):
        return [x_ref[pl.ds(t * OWN * NODES + o, NODES, stride=OWN), :] for o in range(OWN)]

    for i in range(intervals):
        for win, halo, inner in ((w1, 3, 1), (w2, 2, 2), (w3, 1, 3)):
            for o, value in enumerate(source(i * CF + inner)):
                win[i, halo + o] = value
    for o, value in enumerate(source(0)):
        w0[4 + o] = value
    for f in range(4):
        idx[f] = jnp.broadcast_to(nb_ref[f : f + 1, :], (8, PLANE))
    opposite = (1, 0, 3, 2)
    for o in range(OWN):
        for f in range(6):
            row = kinds_ref[f, o : o + 1, :].astype(f32)
            if f < 4:
                wide = jnp.broadcast_to(row, (8, PLANE))
                row = jnp.take_along_axis(wide, idx[opposite[f]], axis=1, mode="promise_in_bounds")[0:1]
            kwin[KH + o, f : f + 1, :] = row
        kwin[KH + o, 6:8, :] = jnp.zeros((2, PLANE), f32)

    count = [0]

    def copy(src, dst, d, ahead):
        k = count[0]
        count[0] += 1
        return pltpu.make_async_remote_copy(
            src_ref=src, dst_ref=dst, send_sem=send_sem.at[k], recv_sem=recv_sem.at[k],
            device_id=at(d, ahead), device_id_type=MESH)

    def swap(win, halo, reach, lead=None):
        made = []
        for d in [s * r for r in range(1, reach + 1) for s in (1, -1)]:
            first, size, skip = span(halo, d)
            src, dst = pl.ds(halo + skip, size), pl.ds(first, size)
            if lead is None:
                made.append(copy(win.at[src], win.at[dst], d, 0))
            else:
                made.append(copy(win.at[lead, src], win.at[lead, dst], d, 0))
        return made

    def hop(block, win, halo, reach):
        made = []
        for d in [0] + [s * r for r in range(1, reach + 1) for s in (1, -1)]:
            first, size, skip = span(halo, d)
            made.append(copy(block.at[pl.ds(skip, size)], win.at[pl.ds(first, size)], d, 1))
        return made

    def start(copies):
        for c in copies:
            c.start()

    def received(copies):
        for c in copies:
            c.wait_recv()

    every = pl.ds(0, intervals)
    swap1 = swap(w1, 3, 2, every)
    swapk = swap(kwin, KH, 2)
    swap2 = swap(w2, 2, 1, every)
    swap3 = swap(w3, 1, 1, every)
    swap0 = swap(w0, 4, 2)
    first_copies = swap1 + swapk + swap2 + swap3 + swap0
    pl.semaphore_wait(barrier, len(partners))
    start(first_copies)

    rows = lax.broadcasted_iota(jnp.int32, (NODES, 2 * NODES), 0)
    cols = lax.broadcasted_iota(jnp.int32, (NODES, 2 * NODES), 1)
    twice = (rows == lax.rem(cols, NODES)).astype(bf16)

    def build(op, volume, faces):
        blocks = [volume[...]] + [faces[f, k] for f in range(6) for k in range(2)]
        for n, block in enumerate(blocks):
            for part, value in enumerate(split(block)):
                op[n * NODES : (n + 1) * NODES, part * 128 : (part + 1) * 128] = dot(value, twice).astype(bf16)

    build(fine_op, fv_ref, ff_ref)
    build(coarse_op, cv_ref, cf_ref)
    index = [jnp.broadcast_to(idx[f, 0:1, :], (NODES, PLANE)) for f in range(4)]

    def inside(z):
        return jnp.logical_and(z >= 0, z < layers)

    def clean(values):
        halo = (len(values) - OWN) // 2
        return [
            v if halo <= l < halo + OWN else jnp.where(inside(sp * OWN - halo + l), v, 0.0)
            for l, v in enumerate(values)
        ]

    def advance(groups, op):
        n = len(groups[0]) - 2
        halo = (n - OWN) // 2
        parts = []
        for values in groups:
            both = [split(v) for v in clean(values)]
            parts.append([jnp.concatenate([h, w, h, w], 0) for h, w in both])
        centre = dot(op[...], jnp.concatenate([v for g in parts for v in g[1:-1]], 1))
        below = dot(op[576:704, :], jnp.concatenate([g[0] for g in parts], 1))
        above = dot(op[704:832, :], jnp.concatenate([g[-1] for g in parts], 1))
        results = []
        for g in range(len(groups)):
            result = []
            for l in range(n):
                def block(b, at_layer=l):
                    c = (g * n + at_layer) * PLANE
                    return centre[b * NODES : (b + 1) * NODES, c : c + PLANE]

                def kind(f):
                    row = kwin[KH - halo + l, f : f + 1, :]
                    return jnp.broadcast_to(row, (NODES, PLANE)) > 0.5

                total = block(0)
                for f in range(4):
                    chosen = jnp.where(kind(f), block(2 + 2 * f), block(1 + 2 * f))
                    total = total + jnp.take_along_axis(chosen, index[f], axis=1, mode="promise_in_bounds")
                here = slice(g * PLANE, (g + 1) * PLANE)
                if l > 0:
                    low = block(9, l - 1), block(10, l - 1)
                else:
                    low = below[:NODES, here], below[NODES:, here]
                if l < n - 1:
                    high = block(11, l + 1), block(12, l + 1)
                else:
                    high = above[:NODES, here], above[NODES:, here]
                total = total + jnp.where(kind(4), low[1], low[0])
                total = total + jnp.where(kind(5), high[1], high[0])
                result.append(total)
            results.append(result)
        return results

    def read(win, halo, keep, i=None):
        rows = range(halo - keep, halo + OWN + keep)
        return [win[r] if i is None else win[i, r] for r in rows]

    def plus(groups, others):
        return [[a + b for a, b in zip(g, h)] for g, h in zip(groups, others)]

    def all_of(win, halo, keep):
        return [read(win, halo, keep, i) for i in range(intervals)]

    received(swap1 + swapk)
    state = advance(all_of(w1, 3, 3), fine_op)
    received(swap2)
    state = plus(state, all_of(w2, 2, 2))
    state = advance(state, fine_op)
    received(swap3)
    state = plus(state, all_of(w3, 1, 1))
    state = advance(state, fine_op)
    for o in range(OWN):
        aout[o] = state[intervals - 1][o]
    hop_a = hop(aout, ain, 4, 2)
    start(hop_a)
    for i in range(1, intervals):
        for o, value in enumerate(source(i * CF)):
            ww[i, 4 + o] = state[i - 1][o] + value
    swap_w = swap(ww, 4, 2, pl.ds(1, intervals - 1))
    start(swap_w)
    received(swap0)
    received(hop_a)
    for l in range(OWN + 8):
        ww[0, l] = w0[l] + jnp.where(tm > 0, ain[l], 0.0)
    received(swap_w)

    state = all_of(ww, 4, 4)
    for _ in range(4):
        state = advance(state, fine_op)
    for o in range(OWN):
        rw0[4 + o] = state[0][o]
        rw1[3 + o] = state[1][o]
        r2[o] = state[2][o]
    swap_r0 = swap(rw0, 4, 2)
    swap_r1 = swap(rw1, 3, 2)
    start(swap_r0 + swap_r1)
    received(swap_r0)
    state = advance([read(rw0, 4, 2)], coarse_op)
    received(swap_r1)
    state = plus(state, [read(rw1, 3, 1)])
    state = advance(state, coarse_op)
    for o in range(OWN):
        lout[o] = state[0][o] + r2[o]

    hop_e = hop(eout, ein, 5, 3)

    @pl.when(tm == 0)
    def _():
        for l in range(OWN + 10):
            ein[l] = jnp.zeros((NODES, PLANE), f32)
        for o in range(OWN):
            eout[o] = lout[o]
        start(hop_e)

    @pl.when(tm > 0)
    def _():
        received(hop_e[:5])

    @pl.when(jnp.logical_and(tm > 0, tm < sections - 1))
    def _():
        state = [read(ein, 5, 3)]
        for _ in range(3):
            state = advance(state, coarse_op)
        for o in range(OWN):
            eout[o] = state[0][o] + lout[o]
        start(hop_e)

    @pl.when(tm > 0)
    def _():
        received(hop_e[5:])

    errors = [read(ein, 5, 5)]
    errors.append(plus(advance([errors[0]], coarse_op), [read(rw0, 4, 4)])[0])
    errors.append(plus(advance([errors[1]], coarse_op), [read(rw1, 3, 3)])[0])
    state = [
        [a + b for a, b in zip(read(ww, 4, 3, i), errors[i][2 - i : 2 - i + OWN + 6])]
        for i in range(intervals)
    ]

    def write(inner, state):
        for i in range(intervals):
            keep = (len(state[i]) - OWN) // 2
            for o in range(OWN):
                t = i * CF + inner
                out_ref[pl.ds(t * OWN * NODES + o, NODES, stride=OWN), :] = state[i][keep + o]

    write(0, state)
    for inner, win, halo, keep in ((1, w1, 3, 2), (2, w2, 2, 1), (3, w3, 1, 0)):
        state = plus(advance(state, fine_op), all_of(win, halo, keep))
        write(inner, state)

    for c in first_copies + hop_a + swap_w + swap_r0 + swap_r1:
        c.wait_send()

    @pl.when(tm < sections - 1)
    def _():
        for c in hop_e:
            c.wait_send()


COPIES = 16 + 5 + 4 + 4 + 4 + 7


def solution(mesh):
    sections, positions = mesh.shape["tm"], mesh.shape["space"]

    def on_device(sources, fine_volume, fine_faces, coarse_volume, coarse_faces, flow_kinds, neighbours):
        steps = sources.shape[0]
        intervals = steps // CF
        layers = OWN * positions

        def body(*refs):
            kernel(sections, positions, layers, intervals, *refs)

        def state(*lead):
            return pltpu.VMEM(lead + (NODES, PLANE), f32)

        vmem = pl.BlockSpec(memory_space=pltpu.VMEM)
        out = pl.pallas_call(
            body,
            out_shape=jax.ShapeDtypeStruct((steps * NODES * OWN, PLANE), f32),
            in_specs=[vmem] * 7,
            out_specs=vmem,
            scratch_shapes=[
                pltpu.VMEM((832, 256), bf16),
                pltpu.VMEM((832, 256), bf16),
                pltpu.VMEM((OWN + 2 * KH, 8, PLANE), f32),
                pltpu.VMEM((4, 8, PLANE), jnp.int32),
                state(OWN + 8),
                state(intervals, OWN + 6),
                state(intervals, OWN + 4),
                state(intervals, OWN + 2),
                state(OWN),
                state(OWN + 8),
                state(intervals, OWN + 8),
                state(OWN + 8),
                state(OWN + 6),
                state(OWN),
                state(OWN),
                state(OWN + 10),
                state(OWN),
                pltpu.SemaphoreType.DMA((COPIES,)),
                pltpu.SemaphoreType.DMA((COPIES,)),
            ],
            compiler_params=pltpu.CompilerParams(
                collective_id=0, has_side_effects=True, vmem_limit_bytes=56 * 1024 * 1024
            ),
        )(sources.reshape(steps * NODES * OWN, PLANE), fine_volume, fine_faces, coarse_volume, coarse_faces,
          flow_kinds, neighbours)
        return out.reshape(sources.shape)

    in_specs = (P("tm", None, "space", None), P(), P(), P(), P(), P(None, "space", None), P())
    out_specs = P("tm", None, "space", None)
    return jax.shard_map(on_device, mesh=mesh, in_specs=in_specs, out_specs=out_specs, check_vma=False)
```

```python
import jax
import jax.numpy as jnp
from jax import lax
from jax.experimental import pallas as pl
from jax.experimental.pallas import tpu as pltpu
from jax.sharding import PartitionSpec as P

CF = 4
NODES = 64
PLANE = 128
OWN = 2
KH = 5
HOST = 1
LAG = 8
MESH = pl.DeviceIdType.MESH
f32, bf16 = jnp.float32, jnp.bfloat16


def dot(a, b):
    return jnp.dot(a, b, preferred_element_type=f32)


def split(value):
    high = value.astype(bf16)
    low = (value - high.astype(f32)).astype(bf16)
    return high, low


def span(halo, d):
    low = halo - OWN * d
    first, last = max(low, 0), min(low + OWN, OWN + 2 * halo)
    return first, last - first, first - low


def kernel(sections, positions, layers, intervals,
           x_ref, fv_ref, ff_ref, cv_ref, cf_ref, kinds_ref, nb_ref, out_ref,
           fine_op, coarse_op, kwin, idx, w0, w1, w2, w3, aout, ain, ww, rw0, rw1, r2, lout, ein, eout,
           pin, pout, terms, chain,
           send_sem, recv_sem, term_send, term_recv, home_send, home_recv, chain_send, chain_recv, token):
    tm, sp = lax.axis_index("tm"), lax.axis_index("space")

    def at(d, ahead):
        return (lax.rem(tm + ahead + sections, sections), lax.rem(sp + d + positions, positions))

    partners = [at(d, 0) for d in (-3, -2, -1, 1, 2, 3)]
    partners += [at(d, a) for a in (-1, 1) for d in range(-3, 4)]
    partners.append((lax.rem(tm + LAG, sections), sp))
    barrier = pltpu.get_barrier_semaphore()
    final = sections - 1

    def greet(device):
        pl.semaphore_signal(barrier, inc=1, device_id=device, device_id_type=MESH)

    for device in partners:
        greet(device)

    @pl.when(tm == HOST)
    def _():
        for s in range(sections):
            if s != HOST:
                greet((s, sp))
        for d in (-3, -2, -1, 1, 2, 3):
            greet((final, at(d, 0)[1]))

    @pl.when(tm != HOST)
    def _():
        greet((HOST, sp))

    @pl.when(tm == final)
    def _():
        for d in (-3, -2, -1, 1, 2, 3):
            greet((HOST, at(d, 0)[1]))

    greetings = len(partners) + jnp.where(tm == HOST, sections - 1 + 6, 1) + jnp.where(tm == final, 6, 0)

    def source(t):
        return [x_ref[pl.ds(t * OWN * NODES + o, NODES, stride=OWN), :] for o in range(OWN)]

    for i in range(intervals):
        for win, halo, inner in ((w1, 3, 1), (w2, 2, 2), (w3, 1, 3)):
            for o, value in enumerate(source(i * CF + inner)):
                win[i, halo + o] = value
    for o, value in enumerate(source(0)):
        w0[4 + o] = value
    for f in range(4):
        idx[f] = jnp.broadcast_to(nb_ref[f : f + 1, :], (8, PLANE))
    opposite = (1, 0, 3, 2)
    for o in range(OWN):
        for f in range(6):
            row = kinds_ref[f, o : o + 1, :].astype(f32)
            if f < 4:
                wide = jnp.broadcast_to(row, (8, PLANE))
                row = jnp.take_along_axis(wide, idx[opposite[f]], axis=1, mode="promise_in_bounds")[0:1]
            kwin[KH + o, f : f + 1, :] = row
        kwin[KH + o, 6:8, :] = jnp.zeros((2, PLANE), f32)

    count = [0]

    def copy(src, dst, d, ahead):
        k = count[0]
        count[0] += 1
        return pltpu.make_async_remote_copy(
            src_ref=src, dst_ref=dst, send_sem=send_sem.at[k], recv_sem=recv_sem.at[k],
            device_id=at(d, ahead), device_id_type=MESH)

    def swap(win, halo, reach, lead=None):
        made = []
        for d in [s * r for r in range(1, reach + 1) for s in (1, -1)]:
            first, size, skip = span(halo, d)
            src, dst = pl.ds(halo + skip, size), pl.ds(first, size)
            if lead is None:
                made.append(copy(win.at[src], win.at[dst], d, 0))
            else:
                made.append(copy(win.at[lead, src], win.at[lead, dst], d, 0))
        return made

    def hop(block, win, halo, reach, ahead=1):
        made = []
        for d in [0] + [s * r for r in range(1, reach + 1) for s in (1, -1)]:
            first, size, skip = span(halo, d)
            made.append(copy(block.at[pl.ds(skip, size)], win.at[pl.ds(first, size)], d, ahead))
        return made

    def start(copies):
        for c in copies:
            c.start()

    def received(copies):
        for c in copies:
            c.wait_recv()

    every = pl.ds(0, intervals)
    swap1 = swap(w1, 3, 2, every)
    swapk = swap(kwin, KH, 3)
    swap2 = swap(w2, 2, 1, every)
    swap3 = swap(w3, 1, 1, every)
    swap0 = swap(w0, 4, 2)
    first_copies = swap1 + swapk + swap2 + swap3 + swap0
    pl.semaphore_wait(barrier, greetings)

    @pl.when(tm >= LAG)
    def _():
        pl.semaphore_wait(token, 1)

    start(swap1 + swapk + swap2 + swap3)

    rows = lax.broadcasted_iota(jnp.int32, (NODES, 2 * NODES), 0)
    cols = lax.broadcasted_iota(jnp.int32, (NODES, 2 * NODES), 1)
    twice = (rows == lax.rem(cols, NODES)).astype(bf16)

    def build(op, volume, faces):
        blocks = [volume[...]] + [faces[f, k] for f in range(6) for k in range(2)]
        for n, block in enumerate(blocks):
            for part, value in enumerate(split(block)):
                op[n * NODES : (n + 1) * NODES, part * 128 : (part + 1) * 128] = dot(value, twice).astype(bf16)

    build(fine_op, fv_ref, ff_ref)
    build(coarse_op, cv_ref, cf_ref)
    index = [jnp.broadcast_to(idx[f, 0:1, :], (NODES, PLANE)) for f in range(4)]

    def inside(z):
        return jnp.logical_and(z >= 0, z < layers)

    def clean(values):
        halo = (len(values) - OWN) // 2
        return [
            v if halo <= l < halo + OWN else jnp.where(inside(sp * OWN - halo + l), v, 0.0)
            for l, v in enumerate(values)
        ]

    def advance(groups, op):
        n = len(groups[0]) - 2
        halo = (n - OWN) // 2
        parts = []
        for values in groups:
            both = [split(v) for v in clean(values)]
            parts.append([jnp.concatenate([h, w, h, w], 0) for h, w in both])
        centre = dot(op[...], jnp.concatenate([v for g in parts for v in g[1:-1]], 1))
        below = dot(op[576:704, :], jnp.concatenate([g[0] for g in parts], 1))
        above = dot(op[704:832, :], jnp.concatenate([g[-1] for g in parts], 1))
        results = []
        for g in range(len(groups)):
            result = []
            for l in range(n):
                def block(b, at_layer=l):
                    c = (g * n + at_layer) * PLANE
                    return centre[b * NODES : (b + 1) * NODES, c : c + PLANE]

                def kind(f):
                    row = kwin[KH - halo + l, f : f + 1, :]
                    return jnp.broadcast_to(row, (NODES, PLANE)) > 0.5

                total = block(0)
                for f in range(4):
                    chosen = jnp.where(kind(f), block(2 + 2 * f), block(1 + 2 * f))
                    total = total + jnp.take_along_axis(chosen, index[f], axis=1, mode="promise_in_bounds")
                here = slice(g * PLANE, (g + 1) * PLANE)
                if l > 0:
                    low = block(9, l - 1), block(10, l - 1)
                else:
                    low = below[:NODES, here], below[NODES:, here]
                if l < n - 1:
                    high = block(11, l + 1), block(12, l + 1)
                else:
                    high = above[:NODES, here], above[NODES:, here]
                total = total + jnp.where(kind(4), low[1], low[0])
                total = total + jnp.where(kind(5), high[1], high[0])
                result.append(total)
            results.append(result)
        return results

    def read(win, halo, keep, i=None):
        rows = range(halo - keep, halo + OWN + keep)
        return [win[r] if i is None else win[i, r] for r in rows]

    def plus(groups, others):
        return [[a + b for a, b in zip(g, h)] for g, h in zip(groups, others)]

    def all_of(win, halo, keep):
        return [read(win, halo, keep, i) for i in range(intervals)]

    received(swap1 + swapk)
    state = advance(all_of(w1, 3, 3), fine_op)
    received(swap2)
    start(swap0)
    state = plus(state, all_of(w2, 2, 2))
    state = advance(state, fine_op)
    received(swap3)
    state = plus(state, all_of(w3, 1, 1))
    state = advance(state, fine_op)
    for o in range(OWN):
        aout[o] = state[intervals - 1][o]
    hop_a = hop(aout, ain, 4, 2)

    @pl.when(tm < final)
    def _():
        start(hop_a)

    for i in range(1, intervals):
        for o, value in enumerate(source(i * CF)):
            ww[i, 4 + o] = state[i - 1][o] + value
    swap_w = swap(ww, 4, 2, pl.ds(1, intervals - 1))
    start(swap_w)
    received(swap0)

    @pl.when(tm == 0)
    def _():
        for l in range(OWN + 8):
            ww[0, l] = w0[l]

    @pl.when(tm > 0)
    def _():
        received(hop_a)
        for l in range(OWN + 8):
            ww[0, l] = w0[l] + ain[l]

    received(swap_w)

    @pl.when(tm < LAG)
    def _():
        pl.semaphore_signal(token, inc=1, device_id=(tm + LAG, sp), device_id_type=MESH)

    state = all_of(ww, 4, 4)
    for _ in range(4):
        state = advance(state, fine_op)
    for o in range(OWN):
        rw0[4 + o] = state[0][o]
        rw1[3 + o] = state[1][o]
        r2[o] = state[2][o]
    swap_r0 = swap(rw0, 4, 2)
    swap_r1 = swap(rw1, 3, 2)
    start(swap_r0 + swap_r1)
    received(swap_r0)
    state = advance([read(rw0, 4, 2)], coarse_op)
    received(swap_r1)
    state = plus(state, [read(rw1, 3, 1)])
    state = advance(state, coarse_op)
    for o in range(OWN):
        lout[o] = state[0][o] + r2[o]

    even = lax.rem(tm, 2) == 0
    hop_l = hop(lout, pin, 3, 2)

    @pl.when(even)
    def _():
        start(hop_l)

    def term(slot):
        return pltpu.make_async_remote_copy(
            src_ref=pout, dst_ref=terms.at[slot], send_sem=term_send, recv_sem=term_recv.at[slot],
            device_id=(HOST, sp), device_id_type=MESH)

    @pl.when(jnp.logical_not(even))
    def _():
        received(hop_l)
        state = [read(pin, 3, 3)]
        for _ in range(3):
            state = advance(state, coarse_op)
        for o in range(OWN):
            pout[o] = state[0][o] + lout[o]

    @pl.when(tm == final - 1)
    def _():
        for o in range(OWN):
            pout[o] = lout[o]

    gives = jnp.logical_or(tm == final - 1, jnp.logical_and(jnp.logical_not(even), jnp.logical_and(tm != HOST, tm < final)))
    slot = (tm + 1) // 2 + jnp.where(even, 0, -1)

    @pl.when(gives)
    def _():
        term(slot).start()

    pairs = sections // 2
    reaches = [s * r for r in (1, 2, 3) for s in (1, -1)]

    def around(side, many=6):
        made = []
        for n, d in enumerate(reaches[:many]):
            first, size, skip = span(6, d)
            made.append(pltpu.make_async_remote_copy(
                src_ref=chain.at[side, pl.ds(6 + skip, size)], dst_ref=chain.at[side, pl.ds(first, size)],
                send_sem=chain_send.at[side, n], recv_sem=chain_recv.at[side, n],
                device_id=at(d, 0), device_id_type=MESH))
        return made

    def home(side, m):
        return pltpu.make_async_remote_copy(
            src_ref=chain.at[side, pl.ds(6, OWN)], dst_ref=ein.at[pl.ds(5, OWN)], send_sem=home_send, recv_sem=home_recv,
            device_id=(2 * m, sp), device_id_type=MESH)

    def wait_term(m):
        term(m).wait_recv()
        return [terms[m, o] for o in range(OWN)]

    hop_f = hop(eout, ein, 5, 3, final - HOST)

    @pl.when(tm == HOST)
    def _():
        for o in range(OWN):
            chain[1, 6 + o] = pout[o]

        def step(m, carry):
            side = lax.rem(m, 2)
            copies = around(side)
            start(copies)
            back = home(side, m)
            back.start()
            received(copies)
            state = [[chain[side, l] for l in range(OWN + 12)]]
            for _ in range(6):
                state = advance(state, coarse_op)
            state = plus(state, [wait_term(m)])
            for o in range(OWN):
                chain[1 - side, 6 + o] = state[0][o]
            for c in copies + [back]:
                c.wait_send()
            return carry

        lax.fori_loop(1, pairs - 1, step, 0)
        side = (pairs - 1) % 2
        copies = around(side, 4)
        start(copies)
        back = home(side, pairs - 1)
        back.start()
        received(copies)
        state = [[chain[side, l] for l in range(3, OWN + 9)]]
        for _ in range(3):
            state = advance(state, coarse_op)
        state = plus(state, [wait_term(pairs - 1)])
        for o in range(OWN):
            eout[o] = state[0][o]
        start(hop_f)
        for c in copies + [back]:
            c.wait_send()

    swap_e = swap(ein, 5, 3)
    hop_e = hop(eout, ein, 5, 3)
    receives = jnp.logical_and(even, tm > 0)
    passes = jnp.logical_and(even, tm < final - 1)

    @pl.when(tm == 0)
    def _():
        for l in range(OWN + 10):
            ein[l] = jnp.zeros((NODES, PLANE), f32)

    @pl.when(receives)
    def _():
        home(0, 0).wait_recv()
        start(swap_e)
        received(swap_e)

    @pl.when(passes)
    def _():
        state = [read(ein, 5, 3)]
        for _ in range(3):
            state = advance(state, coarse_op)
        for o in range(OWN):
            eout[o] = state[0][o] + lout[o]
        start(hop_e)

    @pl.when(jnp.logical_and(jnp.logical_not(even), tm < final))
    def _():
        received(hop_e)

    @pl.when(tm == final)
    def _():
        received(hop_f)

    errors = [read(ein, 5, 5)]
    errors.append(plus(advance([errors[0]], coarse_op), [read(rw0, 4, 4)])[0])
    errors.append(plus(advance([errors[1]], coarse_op), [read(rw1, 3, 3)])[0])
    state = [
        [a + b for a, b in zip(read(ww, 4, 3, i), errors[i][2 - i : 2 - i + OWN + 6])]
        for i in range(intervals)
    ]

    def write(inner, state):
        for i in range(intervals):
            keep = (len(state[i]) - OWN) // 2
            for o in range(OWN):
                t = i * CF + inner
                out_ref[pl.ds(t * OWN * NODES + o, NODES, stride=OWN), :] = state[i][keep + o]

    write(0, state)
    for inner, win, halo, keep in ((1, w1, 3, 2), (2, w2, 2, 1), (3, w3, 1, 0)):
        state = plus(advance(state, fine_op), all_of(win, halo, keep))
        write(inner, state)

    def sent(copies):
        for c in copies:
            c.wait_send()

    sent(first_copies + swap_w + swap_r0 + swap_r1)

    @pl.when(tm < final)
    def _():
        sent(hop_a)

    @pl.when(even)
    def _():
        sent(hop_l)

    @pl.when(gives)
    def _():
        term(slot).wait_send()

    @pl.when(receives)
    def _():
        sent(swap_e)

    @pl.when(passes)
    def _():
        sent(hop_e)

    @pl.when(tm == HOST)
    def _():
        sent(hop_f)


COPIES = 18 + 5 + 4 + 4 + 4 + 5 + 7 + 6 + 7


def solution(mesh):
    sections, positions = mesh.shape["tm"], mesh.shape["space"]

    def on_device(sources, fine_volume, fine_faces, coarse_volume, coarse_faces, flow_kinds, neighbours):
        steps = sources.shape[0]
        intervals = steps // CF
        layers = OWN * positions

        def body(*refs):
            kernel(sections, positions, layers, intervals, *refs)

        def state(*lead):
            return pltpu.VMEM(lead + (NODES, PLANE), f32)

        vmem = pl.BlockSpec(memory_space=pltpu.VMEM)
        out = pl.pallas_call(
            body,
            out_shape=jax.ShapeDtypeStruct((steps * NODES * OWN, PLANE), f32),
            in_specs=[vmem] * 7,
            out_specs=vmem,
            scratch_shapes=[
                pltpu.VMEM((832, 256), bf16),
                pltpu.VMEM((832, 256), bf16),
                pltpu.VMEM((OWN + 2 * KH, 8, PLANE), f32),
                pltpu.VMEM((4, 8, PLANE), jnp.int32),
                state(OWN + 8),
                state(intervals, OWN + 6),
                state(intervals, OWN + 4),
                state(intervals, OWN + 2),
                state(OWN),
                state(OWN + 8),
                state(intervals, OWN + 8),
                state(OWN + 8),
                state(OWN + 6),
                state(OWN),
                state(OWN),
                state(OWN + 10),
                state(OWN),
                state(OWN + 6),
                state(OWN),
                state(sections // 2, OWN),
                state(2, OWN + 12),
                pltpu.SemaphoreType.DMA((COPIES,)),
                pltpu.SemaphoreType.DMA((COPIES,)),
                pltpu.SemaphoreType.DMA,
                pltpu.SemaphoreType.DMA((sections // 2,)),
                pltpu.SemaphoreType.DMA,
                pltpu.SemaphoreType.DMA,
                pltpu.SemaphoreType.DMA((2, 6)),
                pltpu.SemaphoreType.DMA((2, 6)),
                pltpu.SemaphoreType.REGULAR,
            ],
            compiler_params=pltpu.CompilerParams(
                collective_id=0, has_side_effects=True, vmem_limit_bytes=56 * 1024 * 1024
            ),
        )(sources.reshape(steps * NODES * OWN, PLANE), fine_volume, fine_faces, coarse_volume, coarse_faces,
          flow_kinds, neighbours)
        return out.reshape(sources.shape)

    in_specs = (P("tm", None, "space", None), P(), P(), P(), P(), P(None, "space", None), P())
    out_specs = P("tm", None, "space", None)
    return jax.shard_map(on_device, mesh=mesh, in_specs=in_specs, out_specs=out_specs, check_vma=False)
```

```python
import jax
import jax.numpy as jnp
from jax import lax
from jax.experimental import pallas as pl
from jax.experimental.pallas import tpu as pltpu
from jax.sharding import PartitionSpec as P

CF = 4
NODES = 64
PLANE = 128
OWN = 2
KH = 5
MESH = pl.DeviceIdType.MESH
f32, bf16 = jnp.float32, jnp.bfloat16


def dot(a, b):
    return jnp.dot(a, b, preferred_element_type=f32)


def split(value):
    high = value.astype(bf16)
    low = (value - high.astype(f32)).astype(bf16)
    return high, low


def span(halo, d):
    low = halo - OWN * d
    first, last = max(low, 0), min(low + OWN, OWN + 2 * halo)
    return first, last - first, first - low


def kernel(sections, positions, layers, intervals,
           x_ref, fv_ref, ff_ref, cv_ref, cf_ref, kinds_ref, nb_ref, out_ref,
           fine_op, coarse_op, kwin, idx, w1, w2, w3, u2, u3, aout, ain, ww, rw0, rw1, r2, lout, ein,
           pin, pout, terms, chain,
           send_sem, recv_sem, term_send, term_recv, home_send, home_recv, chain_send, chain_recv):
    tm, sp = lax.axis_index("tm"), lax.axis_index("space")

    def at(d, ahead):
        return (lax.rem(tm + ahead + sections, sections), lax.rem(sp + d + positions, positions))

    partners = [at(d, 0) for d in (-3, -2, -1, 1, 2, 3)]
    partners += [at(d, a) for a in (-1, 1) for d in range(-2, 3)]
    barrier = pltpu.get_barrier_semaphore()
    final = sections - 1

    def greet(device):
        pl.semaphore_signal(barrier, inc=1, device_id=device, device_id_type=MESH)

    for device in partners:
        greet(device)

    @pl.when(tm == final)
    def _():
        for s in range(final):
            greet((s, sp))
        for d in (-2, -1, 1, 2):
            greet((1, at(d, 0)[1]))
        for d in (-3, 3):
            greet((0, at(d, 0)[1]))

    @pl.when(tm < final)
    def _():
        greet((final, sp))

    greetings = len(partners) + jnp.where(tm == final, final, 1) + jnp.where(tm == 1, 4, 0) + jnp.where(tm == 0, 2, 0)

    def source(t):
        return [x_ref[pl.ds(t * OWN * NODES + o, NODES, stride=OWN), :] for o in range(OWN)]

    for i in range(intervals):
        for win, halo, inner in ((w1, 2, 1), (w2, 1, 2), (w3, 0, 3)):
            for o, value in enumerate(source(i * CF + inner)):
                win[i, halo + o] = value
    for f in range(4):
        idx[f] = jnp.broadcast_to(nb_ref[f : f + 1, :], (8, PLANE))
    opposite = (1, 0, 3, 2)
    for o in range(OWN):
        for f in range(6):
            row = kinds_ref[f, o : o + 1, :].astype(f32)
            if f < 4:
                wide = jnp.broadcast_to(row, (8, PLANE))
                row = jnp.take_along_axis(wide, idx[opposite[f]], axis=1, mode="promise_in_bounds")[0:1]
            kwin[KH + o, f : f + 1, :] = row
        kwin[KH + o, 6:8, :] = jnp.zeros((2, PLANE), f32)

    count = [0]

    def copy(src, dst, d, ahead):
        k = count[0]
        count[0] += 1
        return pltpu.make_async_remote_copy(
            src_ref=src, dst_ref=dst, send_sem=send_sem.at[k], recv_sem=recv_sem.at[k],
            device_id=at(d, ahead), device_id_type=MESH)

    def swap(win, halo, reach, lead=None):
        made = []
        for d in [s * r for r in range(1, reach + 1) for s in (1, -1)]:
            first, size, skip = span(halo, d)
            src, dst = pl.ds(halo + skip, size), pl.ds(first, size)
            if lead is None:
                made.append(copy(win.at[src], win.at[dst], d, 0))
            else:
                made.append(copy(win.at[lead, src], win.at[lead, dst], d, 0))
        return made

    def layer(win, halo, d, o, lead):
        return copy(win.at[lead, pl.ds(halo + o, 1)], win.at[lead, pl.ds(halo + o - OWN * d, 1)], d, 0)

    def edges(win, halo, lead):
        return [layer(win, halo, 1, OWN - 1, lead), layer(win, halo, -1, 0, lead)]

    def hop(block, win, halo, reach, ahead=1):
        made = []
        for d in [0] + [s * r for r in range(1, reach + 1) for s in (1, -1)]:
            first, size, skip = span(halo, d)
            made.append(copy(block.at[pl.ds(skip, size)], win.at[pl.ds(first, size)], d, ahead))
        return made

    def start(copies):
        for c in copies:
            c.start()

    def received(copies):
        for c in copies:
            c.wait_recv()

    every = pl.ds(0, intervals)
    order = [intervals - 1] + list(range(intervals - 1))
    edges1 = {i: edges(w1, 2, i) for i in order}
    edges2 = {i: edges(u2, 1, i) for i in order}
    edges3 = {i: edges(u3, 1, i) for i in order}
    swapk = swap(kwin, KH, 3)
    pl.semaphore_wait(barrier, greetings)

    start(swapk)
    for i in order:
        start(edges1[i])

    rows = lax.broadcasted_iota(jnp.int32, (NODES, 2 * NODES), 0)
    cols = lax.broadcasted_iota(jnp.int32, (NODES, 2 * NODES), 1)
    twice = (rows == lax.rem(cols, NODES)).astype(bf16)

    def build(op, volume, faces):
        blocks = [volume[...]] + [faces[f, k] for f in range(6) for k in range(2)]
        for n, block in enumerate(blocks):
            for part, value in enumerate(split(block)):
                op[n * NODES : (n + 1) * NODES, part * 128 : (part + 1) * 128] = dot(value, twice).astype(bf16)

    build(fine_op, fv_ref, ff_ref)
    build(coarse_op, cv_ref, cf_ref)
    index = [jnp.broadcast_to(idx[f, 0:1, :], (NODES, PLANE)) for f in range(4)]

    def inside(z):
        return jnp.logical_and(z >= 0, z < layers)

    def clean(values):
        halo = (len(values) - OWN) // 2
        return [
            v if halo <= l < halo + OWN else jnp.where(inside(sp * OWN - halo + l), v, 0.0)
            for l, v in enumerate(values)
        ]

    def advance(groups, op):
        n = len(groups[0]) - 2
        halo = (n - OWN) // 2
        parts = []
        for values in groups:
            both = [split(v) for v in clean(values)]
            parts.append([jnp.concatenate([h, w, h, w], 0) for h, w in both])
        centre = dot(op[...], jnp.concatenate([v for g in parts for v in g[1:-1]], 1))
        below = dot(op[576:704, :], jnp.concatenate([g[0] for g in parts], 1))
        above = dot(op[704:832, :], jnp.concatenate([g[-1] for g in parts], 1))
        results = []
        for g in range(len(groups)):
            result = []
            for l in range(n):
                def block(b, at_layer=l):
                    c = (g * n + at_layer) * PLANE
                    return centre[b * NODES : (b + 1) * NODES, c : c + PLANE]

                def kind(f):
                    row = kwin[KH - halo + l, f : f + 1, :]
                    return jnp.broadcast_to(row, (NODES, PLANE)) > 0.5

                total = block(0)
                for f in range(4):
                    chosen = jnp.where(kind(f), block(2 + 2 * f), block(1 + 2 * f))
                    total = total + jnp.take_along_axis(chosen, index[f], axis=1, mode="promise_in_bounds")
                here = slice(g * PLANE, (g + 1) * PLANE)
                if l > 0:
                    low = block(9, l - 1), block(10, l - 1)
                else:
                    low = below[:NODES, here], below[NODES:, here]
                if l < n - 1:
                    high = block(11, l + 1), block(12, l + 1)
                else:
                    high = above[:NODES, here], above[NODES:, here]
                total = total + jnp.where(kind(4), low[1], low[0])
                total = total + jnp.where(kind(5), high[1], high[0])
                result.append(total)
            results.append(result)
        return results

    def read(win, halo, keep, i=None):
        rows = range(halo - keep, halo + OWN + keep)
        return [win[r] if i is None else win[i, r] for r in rows]

    def plus(groups, others):
        return [[a + b for a, b in zip(g, h)] for g, h in zip(groups, others)]

    def all_of(win, halo, keep):
        return [read(win, halo, keep, i) for i in range(intervals)]

    received(swapk)
    for i in order:
        received(edges1[i])
        state = plus(advance([read(w1, 2, 1, i)], fine_op), [read(w2, 1, 0, i)])[0]
        for o in range(OWN):
            u2[i, 1 + o] = state[o]
        start(edges2[i])
    for i in order:
        received(edges2[i])
        state = plus(advance([read(u2, 1, 1, i)], fine_op), [read(w3, 0, 0, i)])[0]
        for o in range(OWN):
            u3[i, 1 + o] = state[o]
        start(edges3[i])
    hop_a = [copy(aout, ain, 0, 1)]
    for i in order:
        received(edges3[i])
        state = advance([read(u3, 1, 1, i)], fine_op)[0]
        if i == intervals - 1:
            for o in range(OWN):
                aout[o] = state[o]

            @pl.when(tm < final)
            def _():
                start(hop_a)
        else:
            for o, value in enumerate(source((i + 1) * CF)):
                ww[i + 1, 4 + o] = state[o] + value

    swap_w = swap(ww, 4, 2, pl.ds(1, intervals - 1))
    start(swap_w)

    @pl.when(tm == 0)
    def _():
        for o, value in enumerate(source(0)):
            ww[0, 4 + o] = value

    @pl.when(tm > 0)
    def _():
        received(hop_a)
        for o, value in enumerate(source(0)):
            ww[0, 4 + o] = value + ain[o]

    swap_w0 = swap(ww, 4, 2, 0)
    start(swap_w0)
    received(swap_w)
    received(swap_w0)
    late = [layer(w1, 2, 1, 0, every), layer(w1, 2, -1, 1, every)] + edges(w2, 1, every)
    start(late)

    state = all_of(ww, 4, 4)
    for _ in range(4):
        state = advance(state, fine_op)
    for o in range(OWN):
        rw0[4 + o] = state[0][o]
        rw1[3 + o] = state[1][o]
        r2[o] = state[2][o]
    swap_r = swap(rw0, 4, 1) + [
        copy(rw1.at[pl.ds(3 + o, 1)], rw1.at[pl.ds(3 + o - OWN * d, 1)], d, 0) for d, o in ((1, OWN - 1), (-1, 0))]
    start(swap_r)
    received(swap_r[:2])
    state = advance([read(rw0, 4, 2)], coarse_op)
    received(swap_r[2:])
    state = plus(state, [read(rw1, 3, 1)])
    state = advance(state, coarse_op)
    for o in range(OWN):
        lout[o] = state[0][o] + r2[o]

    rest = [copy(rw1.at[pl.ds(3 + o, 1)], rw1.at[pl.ds(3 + o - OWN * d, 1)], d, 0) for d, o in ((1, 0), (-1, 1))]
    for win, halo in ((rw0, 4), (rw1, 3)):
        for d in (2, -2):
            first, size, skip = span(halo, d)
            rest.append(copy(win.at[pl.ds(halo + skip, size)], win.at[pl.ds(first, size)], d, 0))

    even = lax.rem(tm, 2) == 0
    odd = jnp.logical_not(even)
    hop_0 = hop(lout, chain.at[0], 6, 3, -1)
    hop_1 = hop(lout, pin, 3, 2, -2)
    hop_l = hop(lout, pin, 3, 2)
    pairs_up = jnp.logical_and(odd, tm < final)
    gives = jnp.logical_and(even, tm > 0)
    slot = tm // 2 - jnp.where(gives, 1, 0)

    def term(slot):
        return pltpu.make_async_remote_copy(
            src_ref=pout, dst_ref=terms.at[slot], send_sem=term_send, recv_sem=term_recv.at[slot],
            device_id=(final, sp), device_id_type=MESH)

    def sent(copies):
        for c in copies:
            c.wait_send()

    @pl.when(tm == 0)
    def _():
        start(hop_0)
        sent(hop_0)

    @pl.when(tm == 1)
    def _():
        start(hop_1)
        sent(hop_1)

    @pl.when(pairs_up)
    def _():
        start(hop_l)
        sent(hop_l)

    @pl.when(tm == 2)
    def _():
        for o in range(OWN):
            pout[o] = lout[o]
        term(slot).start()
        received(hop_l)

    @pl.when(jnp.logical_and(even, tm > 2))
    def _():
        received(hop_l)
        state = [read(pin, 3, 3)]
        for _ in range(3):
            state = advance(state, coarse_op)
        for o in range(OWN):
            pout[o] = state[0][o] + lout[o]

        term(slot).start()

    @pl.when(gives)
    def _():
        term(slot).wait_send()

    start(rest)

    pairs = sections // 2
    reaches = [s * r for r in (3, 1, 2) for s in (1, -1)]

    def around(side, skip=0):
        made = []
        for n, d in list(enumerate(reaches))[skip:]:
            first, size, lead = span(6, d)
            made.append(pltpu.make_async_remote_copy(
                src_ref=chain.at[side, pl.ds(6 + lead, size)], dst_ref=chain.at[side, pl.ds(first, size)],
                send_sem=chain_send.at[side, n], recv_sem=chain_recv.at[side, n],
                device_id=at(d, 0), device_id_type=MESH))
        return made

    def home(side, m):
        return [
            pltpu.make_async_remote_copy(
                src_ref=chain.at[side, pl.ds(6, OWN)], dst_ref=dst, send_sem=home_send.at[n], recv_sem=home_recv,
                device_id=(2 * m + 1 + n, sp), device_id_type=MESH)
            for n, dst in enumerate((ein.at[pl.ds(5, OWN)], chain.at[0, pl.ds(6, OWN)]))]

    def wait_term(m):
        term(m).wait_recv()
        return [terms[m, o] for o in range(OWN)]

    @pl.when(tm == final)
    def _():
        received(hop_0)
        back = home(0, 0)
        start(back)
        state = [[chain[0, l] for l in range(OWN + 12)]]
        for _ in range(3):
            state = advance(state, coarse_op)
        received(hop_1)
        state = plus(state, [read(pin, 3, 3)])
        for _ in range(3):
            state = advance(state, coarse_op)
        state = plus(state, [wait_term(0)])
        for o in range(OWN):
            chain[1, 6 + o] = state[0][o]
        sent(back)

        def step(m, carry):
            side = lax.rem(m, 2)
            copies = around(side)
            start(copies)
            back = home(side, m)

            @pl.when(m == pairs - 2)
            def _():
                start(back[::-1])

            received(copies)

            @pl.when(m < pairs - 2)
            def _():
                start(back)

            state = [[chain[side, l] for l in range(OWN + 12)]]
            for _ in range(6):
                state = advance(state, coarse_op)
            state = plus(state, [wait_term(m)])
            for o in range(OWN):
                chain[1 - side, 6 + o] = state[0][o]
            sent(copies + back)
            return carry

        lax.fori_loop(1, pairs - 1, step, 0)
        for o in range(OWN):
            ein[5 + o] = chain[(pairs - 1) % 2, 6 + o]

    swap_e = swap(ein, 5, 3)

    @pl.when(tm == 0)
    def _():
        for l in range(OWN + 10):
            ein[l] = jnp.zeros((NODES, PLANE), f32)

    @pl.when(jnp.logical_and(tm > 0, tm < final))
    def _():
        home(0, 0)[0].wait_recv()

    @pl.when(gives)
    def _():
        copies = around(0, 2)
        start(copies)
        received(copies)
        state = [[chain[0, l] for l in range(3, OWN + 9)]]
        for _ in range(3):
            state = advance(state, coarse_op)
        for o in range(OWN):
            ein[5 + o] = state[0][o] + pin[3 + o]
        sent(copies)

    @pl.when(tm > 0)
    def _():
        start(swap_e)
        received(swap_e)

    received(late + rest)
    errors = [read(ein, 5, 5)]
    errors.append(plus(advance([errors[0]], coarse_op), [read(rw0, 4, 4)])[0])
    errors.append(plus(advance([errors[1]], coarse_op), [read(rw1, 3, 3)])[0])
    state = [
        [a + b for a, b in zip(read(ww, 4, 3, i), errors[i][2 - i : 2 - i + OWN + 6])]
        for i in range(intervals)
    ]

    def write(inner, state):
        for i in range(intervals):
            keep = (len(state[i]) - OWN) // 2
            for o in range(OWN):
                t = i * CF + inner
                out_ref[pl.ds(t * OWN * NODES + o, NODES, stride=OWN), :] = state[i][keep + o]

    write(0, state)
    for inner, win, halo, keep in ((1, w1, 2, 2), (2, w2, 1, 1), (3, w3, 0, 0)):
        state = plus(advance(state, fine_op), all_of(win, halo, keep))
        write(inner, state)

    sent([c for group in (edges1, edges2, edges3) for i in order for c in group[i]])
    sent(swapk + swap_w + swap_w0 + swap_r + late + rest)

    @pl.when(tm < final)
    def _():
        sent(hop_a)

    @pl.when(tm > 0)
    def _():
        sent(swap_e)


COPIES = 18 + 6 + 1 + 4 + 4 + 4 + 4 + 6 + 7 + 5 + 5 + 6


def solution(mesh):
    sections, positions = mesh.shape["tm"], mesh.shape["space"]

    def on_device(sources, fine_volume, fine_faces, coarse_volume, coarse_faces, flow_kinds, neighbours):
        steps = sources.shape[0]
        intervals = steps // CF
        layers = OWN * positions

        def body(*refs):
            kernel(sections, positions, layers, intervals, *refs)

        def state(*lead):
            return pltpu.VMEM(lead + (NODES, PLANE), f32)

        vmem = pl.BlockSpec(memory_space=pltpu.VMEM)
        out = pl.pallas_call(
            body,
            out_shape=jax.ShapeDtypeStruct((steps * NODES * OWN, PLANE), f32),
            in_specs=[vmem] * 7,
            out_specs=vmem,
            scratch_shapes=[
                pltpu.VMEM((832, 256), bf16),
                pltpu.VMEM((832, 256), bf16),
                pltpu.VMEM((OWN + 2 * KH, 8, PLANE), f32),
                pltpu.VMEM((4, 8, PLANE), jnp.int32),
                state(intervals, OWN + 4),
                state(intervals, OWN + 2),
                state(intervals, OWN),
                state(intervals, OWN + 2),
                state(intervals, OWN + 2),
                state(OWN),
                state(OWN),
                state(intervals, OWN + 8),
                state(OWN + 8),
                state(OWN + 6),
                state(OWN),
                state(OWN),
                state(OWN + 10),
                state(OWN + 6),
                state(OWN),
                state(sections // 2, OWN),
                state(2, OWN + 12),
                pltpu.SemaphoreType.DMA((COPIES,)),
                pltpu.SemaphoreType.DMA((COPIES,)),
                pltpu.SemaphoreType.DMA,
                pltpu.SemaphoreType.DMA((sections // 2,)),
                pltpu.SemaphoreType.DMA((2,)),
                pltpu.SemaphoreType.DMA,
                pltpu.SemaphoreType.DMA((2, 6)),
                pltpu.SemaphoreType.DMA((2, 6)),
            ],
            compiler_params=pltpu.CompilerParams(
                collective_id=0, has_side_effects=True, vmem_limit_bytes=56 * 1024 * 1024
            ),
        )(sources.reshape(steps * NODES * OWN, PLANE), fine_volume, fine_faces, coarse_volume, coarse_faces,
          flow_kinds, neighbours)
        return out.reshape(sources.shape)

    in_specs = (P("tm", None, "space", None), P(), P(), P(), P(), P(None, "space", None), P())
    out_specs = P("tm", None, "space", None)
    return jax.shard_map(on_device, mesh=mesh, in_specs=in_specs, out_specs=out_specs, check_vma=False)
```

```python
import jax
import jax.numpy as jnp
from jax import lax
from jax.experimental import pallas as pl
from jax.experimental.pallas import tpu as pltpu
from jax.sharding import PartitionSpec as P

CF = 4
NODES = 64
PLANE = 128
OWN = 2
KH = 5
MESH = pl.DeviceIdType.MESH
f32, bf16 = jnp.float32, jnp.bfloat16


def dot(a, b):
    return jnp.dot(a, b, preferred_element_type=f32)


def split(value):
    high = value.astype(bf16)
    low = (value - high.astype(f32)).astype(bf16)
    return high, low


def span(halo, d):
    low = halo - OWN * d
    first, last = max(low, 0), min(low + OWN, OWN + 2 * halo)
    return first, last - first, first - low


def kernel(sections, positions, layers, intervals,
           x_ref, fv_ref, ff_ref, cv_ref, cf_ref, kinds_ref, nb_ref, out_ref,
           fine_op, coarse_op, kwin, idx, w1, w2, w3, u2, u3, aout, ain, ww, rw0, rw1, r2, lout, ein,
           pin, pout, terms, chain,
           send_sem, recv_sem, term_send, term_recv, home_send, home_recv, chain_send, chain_recv):
    tm, sp = lax.axis_index("tm"), lax.axis_index("space")

    def at(d, ahead):
        return (lax.rem(tm + ahead + sections, sections), lax.rem(sp + d + positions, positions))

    partners = [at(d, 0) for d in (-3, -2, -1, 1, 2, 3)]
    partners += [at(d, a) for a in (-1, 1) for d in range(-2, 3)]
    barrier = pltpu.get_barrier_semaphore()
    final = sections - 1

    def greet(device):
        pl.semaphore_signal(barrier, inc=1, device_id=device, device_id_type=MESH)

    for device in partners:
        greet(device)

    @pl.when(tm == final)
    def _():
        for s in range(final):
            greet((s, sp))
        for d in (-2, -1, 1, 2):
            greet((1, at(d, 0)[1]))
        for d in (-3, 3):
            greet((0, at(d, 0)[1]))

    @pl.when(tm < final)
    def _():
        greet((final, sp))

    greetings = len(partners) + jnp.where(tm == final, final, 1) + jnp.where(tm == 1, 4, 0) + jnp.where(tm == 0, 2, 0)

    def source(t):
        return [x_ref[pl.ds(t * OWN * NODES + o, NODES, stride=OWN), :] for o in range(OWN)]

    for i in range(intervals):
        for win, halo, inner in ((w1, 2, 1), (w2, 1, 2), (w3, 0, 3)):
            for o, value in enumerate(source(i * CF + inner)):
                win[i, halo + o] = value
    for f in range(4):
        idx[f] = jnp.broadcast_to(nb_ref[f : f + 1, :], (8, PLANE))
    opposite = (1, 0, 3, 2)
    for o in range(OWN):
        for f in range(6):
            row = kinds_ref[f, o : o + 1, :].astype(f32)
            if f < 4:
                wide = jnp.broadcast_to(row, (8, PLANE))
                row = jnp.take_along_axis(wide, idx[opposite[f]], axis=1, mode="promise_in_bounds")[0:1]
            kwin[KH + o, f : f + 1, :] = row
        kwin[KH + o, 6:8, :] = jnp.zeros((2, PLANE), f32)

    count = [0]

    def copy(src, dst, d, ahead):
        k = count[0]
        count[0] += 1
        return pltpu.make_async_remote_copy(
            src_ref=src, dst_ref=dst, send_sem=send_sem.at[k], recv_sem=recv_sem.at[k],
            device_id=at(d, ahead), device_id_type=MESH)

    def swap(win, halo, reach, lead=None):
        made = []
        for d in [s * r for r in (3, 1, 2) if r <= reach for s in (1, -1)]:
            first, size, skip = span(halo, d)
            src, dst = pl.ds(halo + skip, size), pl.ds(first, size)
            if lead is None:
                made.append(copy(win.at[src], win.at[dst], d, 0))
            else:
                made.append(copy(win.at[lead, src], win.at[lead, dst], d, 0))
        return made

    def layer(win, halo, d, o, lead):
        return copy(win.at[lead, pl.ds(halo + o, 1)], win.at[lead, pl.ds(halo + o - OWN * d, 1)], d, 0)

    def edges(win, halo, lead):
        return [layer(win, halo, 1, OWN - 1, lead), layer(win, halo, -1, 0, lead)]

    def hop(block, win, halo, reach, ahead=1):
        made = []
        for d in [0] + [s * r for r in range(1, reach + 1) for s in (1, -1)]:
            first, size, skip = span(halo, d)
            made.append(copy(block.at[pl.ds(skip, size)], win.at[pl.ds(first, size)], d, ahead))
        return made

    def start(copies):
        for c in copies:
            c.start()

    def received(copies):
        for c in copies:
            c.wait_recv()

    every = pl.ds(0, intervals)
    order = [intervals - 1] + list(range(intervals - 1))
    edges1 = {i: edges(w1, 2, i) for i in order}
    edges2 = {i: edges(u2, 1, i) for i in order}
    edges3 = {i: edges(u3, 1, i) for i in order}
    swapk = swap(kwin, KH, 3)
    pl.semaphore_wait(barrier, greetings)

    for i in order:
        start(edges1[i])
    start(swapk)

    rows = lax.broadcasted_iota(jnp.int32, (NODES, 2 * NODES), 0)
    cols = lax.broadcasted_iota(jnp.int32, (NODES, 2 * NODES), 1)
    twice = (rows == lax.rem(cols, NODES)).astype(bf16)

    def build(op, volume, faces):
        blocks = [volume[...]] + [faces[f, k] for f in range(6) for k in range(2)]
        for n, block in enumerate(blocks):
            for part, value in enumerate(split(block)):
                op[n * NODES : (n + 1) * NODES, part * 128 : (part + 1) * 128] = dot(value, twice).astype(bf16)

    build(fine_op, fv_ref, ff_ref)
    build(coarse_op, cv_ref, cf_ref)
    index = [jnp.broadcast_to(idx[f, 0:1, :], (NODES, PLANE)) for f in range(4)]

    def inside(z):
        return jnp.logical_and(z >= 0, z < layers)

    def clean(values):
        halo = (len(values) - OWN) // 2
        edge = set(range(halo - 1, -1, -OWN)) | set(range(halo + OWN, len(values), OWN))
        return [
            jnp.where(inside(sp * OWN - halo + l), v, 0.0) if l in edge else v
            for l, v in enumerate(values)
        ]

    def advance(groups, op):
        n = len(groups[0]) - 2
        halo = (n - OWN) // 2
        parts = []
        for values in groups:
            both = [split(v) for v in clean(values)]
            parts.append([jnp.concatenate([h, w, h, w], 0) for h, w in both])
        centre = dot(op[...], jnp.concatenate([v for g in parts for v in g[1:-1]], 1))
        below = dot(op[576:704, :], jnp.concatenate([g[0] for g in parts], 1))
        above = dot(op[704:832, :], jnp.concatenate([g[-1] for g in parts], 1))
        results = []
        for g in range(len(groups)):
            result = []
            for l in range(n):
                def block(b, at_layer=l):
                    c = (g * n + at_layer) * PLANE
                    return centre[b * NODES : (b + 1) * NODES, c : c + PLANE]

                def kind(f):
                    row = kwin[KH - halo + l, f : f + 1, :]
                    return jnp.broadcast_to(row, (NODES, PLANE)) > 0.5

                total = block(0)
                for f in range(4):
                    chosen = jnp.where(kind(f), block(2 + 2 * f), block(1 + 2 * f))
                    total = total + jnp.take_along_axis(chosen, index[f], axis=1, mode="promise_in_bounds")
                here = slice(g * PLANE, (g + 1) * PLANE)
                if l > 0:
                    low = block(9, l - 1), block(10, l - 1)
                else:
                    low = below[:NODES, here], below[NODES:, here]
                if l < n - 1:
                    high = block(11, l + 1), block(12, l + 1)
                else:
                    high = above[:NODES, here], above[NODES:, here]
                total = total + jnp.where(kind(4), low[1], low[0])
                total = total + jnp.where(kind(5), high[1], high[0])
                result.append(total)
            results.append(result)
        return results

    def read(win, halo, keep, i=None):
        rows = range(halo - keep, halo + OWN + keep)
        return [win[r] if i is None else win[i, r] for r in rows]

    def plus(groups, others):
        return [[a + b for a, b in zip(g, h)] for g, h in zip(groups, others)]

    def all_of(win, halo, keep):
        return [read(win, halo, keep, i) for i in range(intervals)]

    for i in order:
        received(edges1[i])
        state = plus(advance([read(w1, 2, 1, i)], fine_op), [read(w2, 1, 0, i)])[0]
        for o in range(OWN):
            u2[i, 1 + o] = state[o]
        start(edges2[i])
    for i in order:
        received(edges2[i])
        state = plus(advance([read(u2, 1, 1, i)], fine_op), [read(w3, 0, 0, i)])[0]
        for o in range(OWN):
            u3[i, 1 + o] = state[o]
        start(edges3[i])
    hop_a = [copy(aout, ain, 0, 1)]
    for i in order:
        received(edges3[i])
        state = advance([read(u3, 1, 1, i)], fine_op)[0]
        if i == intervals - 1:
            for o in range(OWN):
                aout[o] = state[o]

            @pl.when(tm < final)
            def _():
                start(hop_a)
        else:
            for o, value in enumerate(source((i + 1) * CF)):
                ww[i + 1, 4 + o] = state[o] + value

    swap_w = swap(ww, 4, 2, pl.ds(1, intervals - 1))
    start(swap_w)

    @pl.when(tm == 0)
    def _():
        for o, value in enumerate(source(0)):
            ww[0, 4 + o] = value

    @pl.when(tm > 0)
    def _():
        received(hop_a)
        for o, value in enumerate(source(0)):
            ww[0, 4 + o] = value + ain[o]

    swap_w0 = swap(ww, 4, 2, 0)
    start(swap_w0)
    received(swap_w)
    received(swap_w0)
    received(swapk)
    late = [layer(w1, 2, 1, 0, every), layer(w1, 2, -1, 1, every)] + edges(w2, 1, every)
    start(late)

    state = all_of(ww, 4, 4)
    for _ in range(4):
        state = advance(state, fine_op)
    for o in range(OWN):
        rw0[4 + o] = state[0][o]
        rw1[3 + o] = state[1][o]
        r2[o] = state[2][o]
    swap_r = swap(rw0, 4, 1) + [
        copy(rw1.at[pl.ds(3 + o, 1)], rw1.at[pl.ds(3 + o - OWN * d, 1)], d, 0) for d, o in ((1, OWN - 1), (-1, 0))]
    start(swap_r)
    received(swap_r[:2])
    state = advance([read(rw0, 4, 2)], coarse_op)
    received(swap_r[2:])
    state = plus(state, [read(rw1, 3, 1)])
    state = advance(state, coarse_op)
    for o in range(OWN):
        lout[o] = state[0][o] + r2[o]

    rest = [copy(rw1.at[pl.ds(3 + o, 1)], rw1.at[pl.ds(3 + o - OWN * d, 1)], d, 0) for d, o in ((1, 0), (-1, 1))]
    for win, halo in ((rw0, 4), (rw1, 3)):
        for d in (2, -2):
            first, size, skip = span(halo, d)
            rest.append(copy(win.at[pl.ds(halo + skip, size)], win.at[pl.ds(first, size)], d, 0))

    even = lax.rem(tm, 2) == 0
    odd = jnp.logical_not(even)
    hop_0 = hop(lout, chain.at[0], 6, 3, -1)
    hop_1 = hop(lout, pin, 3, 2, -2)
    hop_l = hop(lout, pin, 3, 2)
    pairs_up = jnp.logical_and(odd, tm < final)
    gives = jnp.logical_and(even, tm > 0)
    slot = tm // 2 - jnp.where(gives, 1, 0)

    def term(slot):
        return pltpu.make_async_remote_copy(
            src_ref=pout, dst_ref=terms.at[slot], send_sem=term_send, recv_sem=term_recv.at[slot],
            device_id=(final, sp), device_id_type=MESH)

    def sent(copies):
        for c in copies:
            c.wait_send()

    @pl.when(tm == 0)
    def _():
        start(hop_0)
        sent(hop_0)

    @pl.when(tm == 1)
    def _():
        start(hop_1)
        sent(hop_1)

    @pl.when(pairs_up)
    def _():
        start(hop_l)
        sent(hop_l)

    @pl.when(tm == 2)
    def _():
        for o in range(OWN):
            pout[o] = lout[o]
        term(slot).start()
        received(hop_l)

    @pl.when(jnp.logical_and(even, tm > 2))
    def _():
        received(hop_l)
        state = [read(pin, 3, 3)]
        for _ in range(3):
            state = advance(state, coarse_op)
        for o in range(OWN):
            pout[o] = state[0][o] + lout[o]

        term(slot).start()

    @pl.when(gives)
    def _():
        term(slot).wait_send()

    start(rest)

    pairs = sections // 2
    reaches = [s * r for r in (3, 1, 2) for s in (1, -1)]

    def around(side, skip=0):
        made = []
        for n, d in list(enumerate(reaches))[skip:]:
            first, size, lead = span(6, d)
            made.append(pltpu.make_async_remote_copy(
                src_ref=chain.at[side, pl.ds(6 + lead, size)], dst_ref=chain.at[side, pl.ds(first, size)],
                send_sem=chain_send.at[side, n], recv_sem=chain_recv.at[side, n],
                device_id=at(d, 0), device_id_type=MESH))
        return made

    def home(side, m):
        return [
            pltpu.make_async_remote_copy(
                src_ref=chain.at[side, pl.ds(6, OWN)], dst_ref=dst, send_sem=home_send.at[n], recv_sem=home_recv,
                device_id=(2 * m + 1 + n, sp), device_id_type=MESH)
            for n, dst in enumerate((ein.at[pl.ds(5, OWN)], chain.at[0, pl.ds(6, OWN)]))]

    def wait_term(m):
        term(m).wait_recv()
        return [terms[m, o] for o in range(OWN)]

    @pl.when(tm == final)
    def _():
        received(hop_0)
        back = home(0, 0)
        start(back)
        state = [[chain[0, l] for l in range(OWN + 12)]]
        for _ in range(3):
            state = advance(state, coarse_op)
        received(hop_1)
        state = plus(state, [read(pin, 3, 3)])
        for _ in range(3):
            state = advance(state, coarse_op)
        state = plus(state, [wait_term(0)])
        for o in range(OWN):
            chain[1, 6 + o] = state[0][o]
        def step(m, carry):
            side = lax.rem(m, 2)
            copies = around(side)
            start(copies)
            back = home(side, m)
            sent(home(1 - side, m - 1))

            @pl.when(m > 1)
            def _():
                sent(around(1 - side))

            @pl.when(m == pairs - 2)
            def _():
                start(back[::-1])

            received(copies)

            @pl.when(m < pairs - 2)
            def _():
                start(back)

            state = [[chain[side, l] for l in range(OWN + 12)]]
            for _ in range(6):
                state = advance(state, coarse_op)
            state = plus(state, [wait_term(m)])
            for o in range(OWN):
                chain[1 - side, 6 + o] = state[0][o]
            return carry

        lax.fori_loop(1, pairs - 1, step, 0)
        for o in range(OWN):
            ein[5 + o] = chain[(pairs - 1) % 2, 6 + o]

    swap_e = swap(ein, 5, 3)

    @pl.when(tm == 0)
    def _():
        for l in range(OWN + 10):
            ein[l] = jnp.zeros((NODES, PLANE), f32)

    @pl.when(jnp.logical_and(tm > 0, tm < final))
    def _():
        home(0, 0)[0].wait_recv()

    @pl.when(gives)
    def _():
        copies = around(0, 2)
        start(copies)
        received(copies)
        state = [[chain[0, l] for l in range(3, OWN + 9)]]
        for _ in range(3):
            state = advance(state, coarse_op)
        for o in range(OWN):
            ein[5 + o] = state[0][o] + pin[3 + o]
        sent(copies)

    @pl.when(tm > 0)
    def _():
        start(swap_e)
        received(swap_e)

    received(late + rest)
    errors = [read(ein, 5, 5)]
    errors.append(plus(advance([errors[0]], coarse_op), [read(rw0, 4, 4)])[0])
    errors.append(plus(advance([errors[1]], coarse_op), [read(rw1, 3, 3)])[0])
    state = [
        [a + b for a, b in zip(read(ww, 4, 3, i), errors[i][2 - i : 2 - i + OWN + 6])]
        for i in range(intervals)
    ]

    def write(inner, state):
        for i in range(intervals):
            keep = (len(state[i]) - OWN) // 2
            for o in range(OWN):
                t = i * CF + inner
                out_ref[pl.ds(t * OWN * NODES + o, NODES, stride=OWN), :] = state[i][keep + o]

    write(0, state)
    for inner, win, halo, keep in ((1, w1, 2, 2), (2, w2, 1, 1), (3, w3, 0, 0)):
        state = plus(advance(state, fine_op), all_of(win, halo, keep))
        write(inner, state)

    sent([c for group in (edges1, edges2, edges3) for i in order for c in group[i]])
    @pl.when(tm == final)
    def _():
        last = (pairs - 2) % 2
        sent(around(last) + home(last, pairs - 2))

    sent(swapk + swap_w + swap_w0 + swap_r + late + rest)

    @pl.when(tm < final)
    def _():
        sent(hop_a)

    @pl.when(tm > 0)
    def _():
        sent(swap_e)


COPIES = 18 + 6 + 1 + 4 + 4 + 4 + 4 + 6 + 7 + 5 + 5 + 6


def solution(mesh):
    sections, positions = mesh.shape["tm"], mesh.shape["space"]

    def on_device(sources, fine_volume, fine_faces, coarse_volume, coarse_faces, flow_kinds, neighbours):
        steps = sources.shape[0]
        intervals = steps // CF
        layers = OWN * positions

        def body(*refs):
            kernel(sections, positions, layers, intervals, *refs)

        def state(*lead):
            return pltpu.VMEM(lead + (NODES, PLANE), f32)

        vmem = pl.BlockSpec(memory_space=pltpu.VMEM)
        out = pl.pallas_call(
            body,
            out_shape=jax.ShapeDtypeStruct((steps * NODES * OWN, PLANE), f32),
            in_specs=[vmem] * 7,
            out_specs=vmem,
            scratch_shapes=[
                pltpu.VMEM((832, 256), bf16),
                pltpu.VMEM((832, 256), bf16),
                pltpu.VMEM((OWN + 2 * KH, 8, PLANE), f32),
                pltpu.VMEM((4, 8, PLANE), jnp.int32),
                state(intervals, OWN + 4),
                state(intervals, OWN + 2),
                state(intervals, OWN),
                state(intervals, OWN + 2),
                state(intervals, OWN + 2),
                state(OWN),
                state(OWN),
                state(intervals, OWN + 8),
                state(OWN + 8),
                state(OWN + 6),
                state(OWN),
                state(OWN),
                state(OWN + 10),
                state(OWN + 6),
                state(OWN),
                state(sections // 2, OWN),
                state(2, OWN + 12),
                pltpu.SemaphoreType.DMA((COPIES,)),
                pltpu.SemaphoreType.DMA((COPIES,)),
                pltpu.SemaphoreType.DMA,
                pltpu.SemaphoreType.DMA((sections // 2,)),
                pltpu.SemaphoreType.DMA((2,)),
                pltpu.SemaphoreType.DMA,
                pltpu.SemaphoreType.DMA((2, 6)),
                pltpu.SemaphoreType.DMA((2, 6)),
            ],
            compiler_params=pltpu.CompilerParams(
                collective_id=0, has_side_effects=True, vmem_limit_bytes=56 * 1024 * 1024
            ),
        )(sources.reshape(steps * NODES * OWN, PLANE), fine_volume, fine_faces, coarse_volume, coarse_faces,
          flow_kinds, neighbours)
        return out.reshape(sources.shape)

    in_specs = (P("tm", None, "space", None), P(), P(), P(), P(), P(None, "space", None), P())
    out_specs = P("tm", None, "space", None)
    return jax.shard_map(on_device, mesh=mesh, in_specs=in_specs, out_specs=out_specs, check_vma=False)
```

```python
import jax
import jax.numpy as jnp
from jax import lax
from jax.experimental import pallas as pl
from jax.experimental.pallas import tpu as pltpu
from jax.sharding import PartitionSpec as P

CF = 4
NODES = 64
PLANE = 128
OWN = 2
KH = 5
MESH = pl.DeviceIdType.MESH
f32, bf16 = jnp.float32, jnp.bfloat16


def dot(a, b):
    return jnp.dot(a, b, preferred_element_type=f32)


def split(value):
    high = value.astype(bf16)
    low = (value - high.astype(f32)).astype(bf16)
    return high, low


def span(halo, d):
    low = halo - OWN * d
    first, last = max(low, 0), min(low + OWN, OWN + 2 * halo)
    return first, last - first, first - low


def kernel(sections, positions, layers, intervals,
           x_ref, fv_ref, ff_ref, cv_ref, cf_ref, kinds_ref, nb_ref, out_ref,
           fine_op, coarse_op, kwin, idx, w1, w2, w3, u2, u3, aout, ain, ww, rw0, rw1, r2, lout, ein,
           pin, pout, terms, chain,
           send_sem, recv_sem, term_send, term_recv, home_send, home_recv, chain_send, chain_recv):
    tm, sp = lax.axis_index("tm"), lax.axis_index("space")

    def at(d, ahead):
        return (lax.rem(tm + ahead + sections, sections), lax.rem(sp + d + positions, positions))

    partners = [at(d, 0) for d in (-3, -2, -1, 1, 2, 3)]
    partners += [at(d, a) for a in (-1, 1) for d in range(-2, 3)]
    barrier = pltpu.get_barrier_semaphore()
    final = sections - 1

    def greet(device):
        pl.semaphore_signal(barrier, inc=1, device_id=device, device_id_type=MESH)

    for device in partners:
        greet(device)

    @pl.when(tm == final)
    def _():
        for s in range(final):
            greet((s, sp))
        for d in (-2, -1, 1, 2):
            greet((1, at(d, 0)[1]))
        for d in (-3, 3):
            greet((0, at(d, 0)[1]))

    @pl.when(tm < final)
    def _():
        greet((final, sp))

    greetings = len(partners) + jnp.where(tm == final, final, 1) + jnp.where(tm == 1, 4, 0) + jnp.where(tm == 0, 2, 0)

    def source(t):
        return [x_ref[pl.ds(t * OWN * NODES + o, NODES, stride=OWN), :] for o in range(OWN)]

    for i in range(intervals):
        for win, halo, inner in ((w1, 2, 1), (w2, 1, 2), (w3, 0, 3)):
            for o, value in enumerate(source(i * CF + inner)):
                win[i, halo + o] = value
    for f in range(4):
        idx[f] = jnp.broadcast_to(nb_ref[f : f + 1, :], (8, PLANE))
    opposite = (1, 0, 3, 2)
    for o in range(OWN):
        for f in range(6):
            row = kinds_ref[f, o : o + 1, :].astype(f32)
            if f < 4:
                wide = jnp.broadcast_to(row, (8, PLANE))
                row = jnp.take_along_axis(wide, idx[opposite[f]], axis=1, mode="promise_in_bounds")[0:1]
            kwin[KH + o, f : f + 1, :] = row
        kwin[KH + o, 6:8, :] = jnp.zeros((2, PLANE), f32)

    count = [0]

    def copy(src, dst, d, ahead):
        k = count[0]
        count[0] += 1
        return pltpu.make_async_remote_copy(
            src_ref=src, dst_ref=dst, send_sem=send_sem.at[k], recv_sem=recv_sem.at[k],
            device_id=at(d, ahead), device_id_type=MESH)

    def swap(win, halo, reach, lead=None):
        made = []
        for d in [s * r for r in (3, 1, 2) if r <= reach for s in (1, -1)]:
            first, size, skip = span(halo, d)
            src, dst = pl.ds(halo + skip, size), pl.ds(first, size)
            if lead is None:
                made.append(copy(win.at[src], win.at[dst], d, 0))
            else:
                made.append(copy(win.at[lead, src], win.at[lead, dst], d, 0))
        return made

    def layer(win, halo, d, o, lead):
        return copy(win.at[lead, pl.ds(halo + o, 1)], win.at[lead, pl.ds(halo + o - OWN * d, 1)], d, 0)

    def edges(win, halo, lead):
        return [layer(win, halo, 1, OWN - 1, lead), layer(win, halo, -1, 0, lead)]

    def hop(block, win, halo, reach, ahead=1):
        made = []
        for d in [0] + [s * r for r in range(1, reach + 1) for s in (1, -1)]:
            first, size, skip = span(halo, d)
            made.append(copy(block.at[pl.ds(skip, size)], win.at[pl.ds(first, size)], d, ahead))
        return made

    def start(copies):
        for c in copies:
            c.start()

    def received(copies):
        for c in copies:
            c.wait_recv()

    every = pl.ds(0, intervals)
    order = [intervals - 1] + list(range(intervals - 1))
    edges1 = {i: edges(w1, 2, i) for i in order}
    edges2 = {i: edges(u2, 1, i) for i in order}
    edges3 = {i: edges(u3, 1, i) for i in order}
    swapk = swap(kwin, KH, 3)
    pl.semaphore_wait(barrier, greetings)

    for i in order:
        start(edges1[i])
    start(swapk)

    rows = lax.broadcasted_iota(jnp.int32, (NODES, 2 * NODES), 0)
    cols = lax.broadcasted_iota(jnp.int32, (NODES, 2 * NODES), 1)
    twice = (rows == lax.rem(cols, NODES)).astype(bf16)

    def build(op, volume, faces):
        blocks = [volume[...]] + [faces[f, k] for f in range(6) for k in range(2)]
        for n, block in enumerate(blocks):
            for part, value in enumerate(split(block)):
                op[n * NODES : (n + 1) * NODES, part * 128 : (part + 1) * 128] = dot(value, twice).astype(bf16)

    build(fine_op, fv_ref, ff_ref)
    build(coarse_op, cv_ref, cf_ref)
    index = [jnp.broadcast_to(idx[f, 0:1, :], (NODES, PLANE)) for f in range(4)]

    def inside(z):
        return jnp.logical_and(z >= 0, z < layers)

    def clean(values):
        halo = (len(values) - OWN) // 2
        edge = set(range(halo - 1, -1, -OWN)) | set(range(halo + OWN, len(values), OWN))
        return [
            jnp.where(inside(sp * OWN - halo + l), v, 0.0) if l in edge else v
            for l, v in enumerate(values)
        ]

    def advance(groups, op):
        n = len(groups[0]) - 2
        halo = (n - OWN) // 2
        parts = []
        for values in groups:
            both = [split(v) for v in clean(values)]
            parts.append([jnp.concatenate([h, w, h, w], 0) for h, w in both])
        centre = dot(op[...], jnp.concatenate([v for g in parts for v in g[1:-1]], 1))
        below = dot(op[576:704, :], jnp.concatenate([g[0] for g in parts], 1))
        above = dot(op[704:832, :], jnp.concatenate([g[-1] for g in parts], 1))
        results = []
        for g in range(len(groups)):
            result = []
            for l in range(n):
                def block(b, at_layer=l):
                    c = (g * n + at_layer) * PLANE
                    return centre[b * NODES : (b + 1) * NODES, c : c + PLANE]

                def kind(f):
                    row = kwin[KH - halo + l, f : f + 1, :]
                    return jnp.broadcast_to(row, (NODES, PLANE)) > 0.5

                total = block(0)
                for f in range(4):
                    chosen = jnp.where(kind(f), block(2 + 2 * f), block(1 + 2 * f))
                    total = total + jnp.take_along_axis(chosen, index[f], axis=1, mode="promise_in_bounds")
                here = slice(g * PLANE, (g + 1) * PLANE)
                if l > 0:
                    low = block(9, l - 1), block(10, l - 1)
                else:
                    low = below[:NODES, here], below[NODES:, here]
                if l < n - 1:
                    high = block(11, l + 1), block(12, l + 1)
                else:
                    high = above[:NODES, here], above[NODES:, here]
                total = total + jnp.where(kind(4), low[1], low[0])
                total = total + jnp.where(kind(5), high[1], high[0])
                result.append(total)
            results.append(result)
        return results

    def read(win, halo, keep, i=None):
        rows = range(halo - keep, halo + OWN + keep)
        return [win[r] if i is None else win[i, r] for r in rows]

    def plus(groups, others):
        return [[a + b for a, b in zip(g, h)] for g, h in zip(groups, others)]

    def all_of(win, halo, keep):
        return [read(win, halo, keep, i) for i in range(intervals)]

    for i in order:
        received(edges1[i])
        state = plus(advance([read(w1, 2, 1, i)], fine_op), [read(w2, 1, 0, i)])[0]
        for o in range(OWN):
            u2[i, 1 + o] = state[o]
        start(edges2[i])
    for i in order:
        received(edges2[i])
        state = plus(advance([read(u2, 1, 1, i)], fine_op), [read(w3, 0, 0, i)])[0]
        for o in range(OWN):
            u3[i, 1 + o] = state[o]
        start(edges3[i])
    hop_a = [copy(aout, ain, 0, 1)]
    for i in order:
        received(edges3[i])
        state = advance([read(u3, 1, 1, i)], fine_op)[0]
        if i == intervals - 1:
            for o in range(OWN):
                aout[o] = state[o]

            @pl.when(tm < final)
            def _():
                start(hop_a)
        else:
            for o, value in enumerate(source((i + 1) * CF)):
                ww[i + 1, 4 + o] = state[o] + value

    swap_w = swap(ww, 4, 2, pl.ds(1, intervals - 1))
    start(swap_w)

    @pl.when(tm == 0)
    def _():
        for o, value in enumerate(source(0)):
            ww[0, 4 + o] = value

    @pl.when(tm > 0)
    def _():
        received(hop_a)
        for o, value in enumerate(source(0)):
            ww[0, 4 + o] = value + ain[o]

    swap_w0 = swap(ww, 4, 2, 0)
    start(swap_w0)
    received(swap_w)
    received(swap_w0)
    received(swapk)
    late = [layer(w1, 2, 1, 0, every), layer(w1, 2, -1, 1, every)] + edges(w2, 1, every)

    @pl.when(tm >= sections - 2)
    def _():
        start(late)


    state = all_of(ww, 4, 4)
    for _ in range(4):
        state = advance(state, fine_op)
    for o in range(OWN):
        rw0[4 + o] = state[0][o]
        rw1[3 + o] = state[1][o]
        r2[o] = state[2][o]
    swap_r = swap(rw0, 4, 1) + [
        copy(rw1.at[pl.ds(3 + o, 1)], rw1.at[pl.ds(3 + o - OWN * d, 1)], d, 0) for d, o in ((1, OWN - 1), (-1, 0))]
    start(swap_r)
    received(swap_r[:2])
    state = advance([read(rw0, 4, 2)], coarse_op)
    received(swap_r[2:])
    state = plus(state, [read(rw1, 3, 1)])
    state = advance(state, coarse_op)
    for o in range(OWN):
        lout[o] = state[0][o] + r2[o]

    rest = [copy(rw1.at[pl.ds(3 + o, 1)], rw1.at[pl.ds(3 + o - OWN * d, 1)], d, 0) for d, o in ((1, 0), (-1, 1))]
    for win, halo in ((rw0, 4), (rw1, 3)):
        for d in (2, -2):
            first, size, skip = span(halo, d)
            rest.append(copy(win.at[pl.ds(halo + skip, size)], win.at[pl.ds(first, size)], d, 0))

    even = lax.rem(tm, 2) == 0
    odd = jnp.logical_not(even)
    hop_0 = hop(lout, chain.at[0], 6, 3, -1)
    hop_1 = hop(lout, pin, 3, 2, -2)
    hop_l = hop(lout, pin, 3, 2)
    pairs_up = jnp.logical_and(odd, tm < final)
    gives = jnp.logical_and(even, tm > 0)
    slot = tm // 2 - jnp.where(gives, 1, 0)

    def term(slot):
        return pltpu.make_async_remote_copy(
            src_ref=pout, dst_ref=terms.at[slot], send_sem=term_send, recv_sem=term_recv.at[slot],
            device_id=(final, sp), device_id_type=MESH)

    def sent(copies):
        for c in copies:
            c.wait_send()

    @pl.when(tm == 0)
    def _():
        start(hop_0)
        sent(hop_0)

    @pl.when(tm == 1)
    def _():
        start(hop_1)
        sent(hop_1)

    @pl.when(pairs_up)
    def _():
        start(hop_l)
        sent(hop_l)

    @pl.when(tm == 2)
    def _():
        for o in range(OWN):
            pout[o] = lout[o]
        term(slot).start()
        received(hop_l)

    @pl.when(jnp.logical_and(even, tm > 2))
    def _():
        received(hop_l)
        state = [read(pin, 3, 3)]
        for _ in range(3):
            state = advance(state, coarse_op)
        for o in range(OWN):
            pout[o] = state[0][o] + lout[o]

        term(slot).start()

    @pl.when(gives)
    def _():
        term(slot).wait_send()

    start(rest)

    @pl.when(tm < sections - 2)
    def _():
        start(late)

    pairs = sections // 2
    reaches = [s * r for r in (3, 1, 2) for s in (1, -1)]

    def around(side, skip=0):
        made = []
        for n, d in list(enumerate(reaches))[skip:]:
            first, size, lead = span(6, d)
            made.append(pltpu.make_async_remote_copy(
                src_ref=chain.at[side, pl.ds(6 + lead, size)], dst_ref=chain.at[side, pl.ds(first, size)],
                send_sem=chain_send.at[side, n], recv_sem=chain_recv.at[side, n],
                device_id=at(d, 0), device_id_type=MESH))
        return made

    def home(side, m):
        return [
            pltpu.make_async_remote_copy(
                src_ref=chain.at[side, pl.ds(6, OWN)], dst_ref=dst, send_sem=home_send.at[n], recv_sem=home_recv,
                device_id=(2 * m + 1 + n, sp), device_id_type=MESH)
            for n, dst in enumerate((ein.at[pl.ds(5, OWN)], chain.at[0, pl.ds(6, OWN)]))]

    def wait_term(m):
        term(m).wait_recv()
        return [terms[m, o] for o in range(OWN)]

    @pl.when(tm == final)
    def _():
        received(hop_0)
        back = home(0, 0)
        start(back)
        state = [[chain[0, l] for l in range(OWN + 12)]]
        for _ in range(3):
            state = advance(state, coarse_op)
        received(hop_1)
        state = plus(state, [read(pin, 3, 3)])
        for _ in range(3):
            state = advance(state, coarse_op)
        state = plus(state, [wait_term(0)])
        for o in range(OWN):
            chain[1, 6 + o] = state[0][o]
        def step(m, carry):
            side = lax.rem(m, 2)
            copies = around(side)
            start(copies)
            back = home(side, m)
            sent(home(1 - side, m - 1))

            @pl.when(m > 1)
            def _():
                sent(around(1 - side))

            @pl.when(m == pairs - 2)
            def _():
                start(back[::-1])

            received(copies)

            @pl.when(m < pairs - 2)
            def _():
                start(back)

            state = [[chain[side, l] for l in range(OWN + 12)]]
            for _ in range(6):
                state = advance(state, coarse_op)
            state = plus(state, [wait_term(m)])
            for o in range(OWN):
                chain[1 - side, 6 + o] = state[0][o]
            return carry

        lax.fori_loop(1, pairs - 1, step, 0)
        for o in range(OWN):
            ein[5 + o] = chain[(pairs - 1) % 2, 6 + o]

    swap_e = swap(ein, 5, 3)

    @pl.when(tm == 0)
    def _():
        for l in range(OWN + 10):
            ein[l] = jnp.zeros((NODES, PLANE), f32)

    @pl.when(jnp.logical_and(tm > 0, tm < final))
    def _():
        home(0, 0)[0].wait_recv()

    @pl.when(gives)
    def _():
        copies = around(0, 2)
        start(copies)
        received(copies)
        state = [[chain[0, l] for l in range(3, OWN + 9)]]
        for _ in range(3):
            state = advance(state, coarse_op)
        for o in range(OWN):
            ein[5 + o] = state[0][o] + pin[3 + o]
        sent(copies)

    @pl.when(tm > 0)
    def _():
        start(swap_e)
        received(swap_e)

    received(late + rest)
    errors = [read(ein, 5, 5)]
    errors.append(plus(advance([errors[0]], coarse_op), [read(rw0, 4, 4)])[0])
    errors.append(plus(advance([errors[1]], coarse_op), [read(rw1, 3, 3)])[0])
    state = [
        [a + b for a, b in zip(read(ww, 4, 3, i), errors[i][2 - i : 2 - i + OWN + 6])]
        for i in range(intervals)
    ]

    def write(inner, state):
        for i in range(intervals):
            keep = (len(state[i]) - OWN) // 2
            for o in range(OWN):
                t = i * CF + inner
                out_ref[pl.ds(t * OWN * NODES + o, NODES, stride=OWN), :] = state[i][keep + o]

    write(0, state)
    for inner, win, halo, keep in ((1, w1, 2, 2), (2, w2, 1, 1), (3, w3, 0, 0)):
        state = plus(advance(state, fine_op), all_of(win, halo, keep))
        write(inner, state)

    sent([c for group in (edges1, edges2, edges3) for i in order for c in group[i]])
    @pl.when(tm == final)
    def _():
        last = (pairs - 2) % 2
        sent(around(last) + home(last, pairs - 2))

    sent(swapk + swap_w + swap_w0 + swap_r + late + rest)

    @pl.when(tm < final)
    def _():
        sent(hop_a)

    @pl.when(tm > 0)
    def _():
        sent(swap_e)


COPIES = 18 + 6 + 1 + 4 + 4 + 4 + 4 + 6 + 7 + 5 + 5 + 6


def solution(mesh):
    sections, positions = mesh.shape["tm"], mesh.shape["space"]

    def on_device(sources, fine_volume, fine_faces, coarse_volume, coarse_faces, flow_kinds, neighbours):
        steps = sources.shape[0]
        intervals = steps // CF
        layers = OWN * positions

        def body(*refs):
            kernel(sections, positions, layers, intervals, *refs)

        def state(*lead):
            return pltpu.VMEM(lead + (NODES, PLANE), f32)

        vmem = pl.BlockSpec(memory_space=pltpu.VMEM)
        out = pl.pallas_call(
            body,
            out_shape=jax.ShapeDtypeStruct((steps * NODES * OWN, PLANE), f32),
            in_specs=[vmem] * 7,
            out_specs=vmem,
            scratch_shapes=[
                pltpu.VMEM((832, 256), bf16),
                pltpu.VMEM((832, 256), bf16),
                pltpu.VMEM((OWN + 2 * KH, 8, PLANE), f32),
                pltpu.VMEM((4, 8, PLANE), jnp.int32),
                state(intervals, OWN + 4),
                state(intervals, OWN + 2),
                state(intervals, OWN),
                state(intervals, OWN + 2),
                state(intervals, OWN + 2),
                state(OWN),
                state(OWN),
                state(intervals, OWN + 8),
                state(OWN + 8),
                state(OWN + 6),
                state(OWN),
                state(OWN),
                state(OWN + 10),
                state(OWN + 6),
                state(OWN),
                state(sections // 2, OWN),
                state(2, OWN + 12),
                pltpu.SemaphoreType.DMA((COPIES,)),
                pltpu.SemaphoreType.DMA((COPIES,)),
                pltpu.SemaphoreType.DMA,
                pltpu.SemaphoreType.DMA((sections // 2,)),
                pltpu.SemaphoreType.DMA((2,)),
                pltpu.SemaphoreType.DMA,
                pltpu.SemaphoreType.DMA((2, 6)),
                pltpu.SemaphoreType.DMA((2, 6)),
            ],
            compiler_params=pltpu.CompilerParams(
                collective_id=0, has_side_effects=True, vmem_limit_bytes=56 * 1024 * 1024
            ),
        )(sources.reshape(steps * NODES * OWN, PLANE), fine_volume, fine_faces, coarse_volume, coarse_faces,
          flow_kinds, neighbours)
        return out.reshape(sources.shape)

    in_specs = (P("tm", None, "space", None), P(), P(), P(), P(), P(None, "space", None), P())
    out_specs = P("tm", None, "space", None)
    return jax.shard_map(on_device, mesh=mesh, in_specs=in_specs, out_specs=out_specs, check_vma=False)
```
